512 devices in a mesh: node: 16 (over x, z_lo), group: 32 (over y, z_hi, core).
Axes of the slice: x: 4, y: 8, z: 8 (z_hi: 2, z_lo: 4; z = z_hi * 4 + z_lo), core: 2. Of those that a mesh axis runs over, the one named last changes fastest.
Arguments:
- queries: bfloat16 [32, 2048, 128], P('group', 'node'), may hold values from -6 to 6
- keys: bfloat16 [32, 2048, 128], P('group', 'node'), may hold values from -6 to 6
- values: bfloat16 [32, 2048, 128], P('group', 'node'), may hold values from -6 to 6
- out_grad: bfloat16 [32, 2048, 12288], P('group', 'node'), may hold values from -6 to 6
- out_weight: bfloat16 [128, 12288], P(None, 'node'), may hold values from -0.0546875 to 0.0546875
- block_offsets: int32 [129], replicated, may hold values from 0 to 1626112, as said below
Outputs:
- bucket: float32 [1638400], P(('node', 'group'))
- qkv_grads: bfloat16 [32, 2048, 384], P('group', 'node')
The draws below stay inside these ranges and needn't reach their ends.
Inputs may be any that keep to these rules, and one draw needn't show every extreme that they name: block_offsets[b] is a multiple of 128 and block_offsets[b + 1] >= block_offsets[b] + 12288.
All inputs are finite; a program needn't handle non-finite values.
Results may differ from the reference program's by a relative error of at most 0.02.
Values may be sent and summed in bfloat16 or wider, within the bound.
A program may use at most 64 MiB of HBM per device.

```python
import math
import jax
import jax.numpy as jnp
from jax import lax

D = 12288
HD = 128
TOK_DEV = 128
BAND = 128
SEQS = 32
LENGTH = 2048
TOKENS = 65536
BLOCKS = 129
DR = 96
FR = 12800
FLAT = 1638400
N_NODE = 16


def draw_queries(key, part):
    key = jax.random.fold_in(key, 21)
    result = jnp.clip(jax.random.normal(key, (SEQS, LENGTH, HD), jnp.float32), -6.0, 6.0)
    return result.astype(jnp.bfloat16)


def draw_keys(key, part):
    key = jax.random.fold_in(key, 22)
    result = jnp.clip(jax.random.normal(key, (SEQS, LENGTH, HD), jnp.float32), -6.0, 6.0)
    return result.astype(jnp.bfloat16)


def draw_block_offsets(key, part):
    key = jax.random.fold_in(key, 11)
    spare = FR - BLOCKS * DR
    cuts = jnp.sort(jax.random.randint(key, (BLOCKS,), 0, spare + 1))
    cuts = cuts.at[0].set(0).at[BLOCKS - 1].set(spare)
    return ((jnp.arange(BLOCKS) * DR + cuts) * 128).astype(jnp.int32)


def block_levels(rng, shape, pieces, smallest, largest):
    loudness, own = 1.0, jax.random.fold_in(rng, 6)
    for axis_at, shards_of in pieces:
        draws = jnp.exp(jax.random.uniform(jax.random.fold_in(own, axis_at), (shards_of,), jnp.float32, smallest / len(pieces), largest / len(pieces)))
        loudness = loudness * jnp.repeat(draws, shape[axis_at] // shards_of).reshape([-1 if axis == axis_at else 1 for axis in range(len(shape))])
    return loudness


def centred(key, shape, deviation, most, shards=(), held_as=jnp.bfloat16):
    drawn = deviation * jax.random.normal(key, shape, jnp.float32)
    if shards:
        drawn = drawn * block_levels(key, shape, shards, -0.22, 0.18)
    return jnp.clip(drawn, -most, most).astype(held_as)


def setup_inputs(seed: int = 0) -> dict:
    arg_keys = jax.random.split(jax.random.key(seed), 7)
    return {
        "queries": draw_queries(jax.random.fold_in(arg_keys[6], 71), 0),
        "keys": draw_keys(jax.random.fold_in(arg_keys[6], 71), 0),
        "values": centred(arg_keys[2], (SEQS, LENGTH, HD), 1.0, 6.0, ((0, 32), (1, 16))),
        "out_grad": centred(arg_keys[3], (SEQS, LENGTH, D), 1.0, 6.0, ((0, 32), (1, 16))),
        "out_weight": centred(arg_keys[4], (HD, D), D ** -0.5, 0.0546875, ((1, 16),)),
        "block_offsets": draw_block_offsets(jax.random.fold_in(arg_keys[6], 71), 0),
    }


def lay_rows(grads_rows, off_rows, flat_rows, per_block):
    below = off_rows[None, :] <= flat_rows[:, None]
    starts = lax.optimization_barrier(jnp.max(jnp.where(below, off_rows[None, :], -1), axis=1))
    index = lax.optimization_barrier(jnp.sum(below.astype(jnp.int32), axis=1)) - 1
    within = flat_rows - starts
    valid = (index >= 0) & (within < per_block)
    source = jnp.where(valid, index * per_block + within, 0).astype(jnp.int32)
    picked = jnp.take(grads_rows, source, axis=0)
    return jnp.where(valid[:, None], picked, jnp.zeros_like(picked))

def reference(queries, keys, values, out_grad, out_weight, block_offsets):
    scale = 1.0 / math.sqrt(HD)
    place = jnp.arange(LENGTH)
    allowed = (place[None, :] <= place[:, None]) & (place[None, :] > place[:, None] - BAND)

    def one_seq(total, items):
        query, key_seq, value, cot = items
        scores = jnp.dot(query, key_seq.T, preferred_element_type=jnp.float32) * scale
        scores = jnp.where(allowed, scores, -jnp.inf)
        top = lax.optimization_barrier(jnp.max(scores, axis=1, keepdims=True))
        expo = jnp.exp(scores - top)
        probs = expo / lax.optimization_barrier(jnp.sum(expo, axis=1, keepdims=True))
        probs_low = probs.astype(jnp.bfloat16)
        attended = jnp.dot(probs_low, value, preferred_element_type=jnp.float32).astype(jnp.bfloat16)
        head_grad = jnp.dot(cot, out_weight.T, preferred_element_type=jnp.float32)
        head_low = head_grad.astype(jnp.bfloat16)
        prob_grad = jnp.dot(head_low, value.T, preferred_element_type=jnp.float32)
        center = lax.optimization_barrier(jnp.sum(probs * prob_grad, axis=1, keepdims=True))
        score_grad = (probs * (prob_grad - center) * scale).astype(jnp.bfloat16)
        grad_q = jnp.dot(score_grad, key_seq, preferred_element_type=jnp.float32).astype(jnp.bfloat16)
        grad_k = jnp.dot(score_grad.T, query, preferred_element_type=jnp.float32).astype(jnp.bfloat16)
        grad_v = jnp.dot(probs_low.T, head_low, preferred_element_type=jnp.float32).astype(jnp.bfloat16)
        att_blocks = attended.reshape(N_NODE, TOK_DEV, HD).astype(jnp.float32)
        cot_blocks = cot.reshape(N_NODE, TOK_DEV, D).astype(jnp.float32)
        weight_terms = jnp.einsum('nrh,nrd->nhd', att_blocks, cot_blocks)
        weight_terms = lax.optimization_barrier(weight_terms.astype(jnp.bfloat16)).astype(jnp.float32)
        bias_terms = lax.optimization_barrier(jnp.sum(cot_blocks, axis=1))
        bias_terms = lax.optimization_barrier(bias_terms.astype(jnp.bfloat16)).astype(jnp.float32)
        summed = jnp.concatenate([lax.optimization_barrier(jnp.sum(weight_terms, axis=0)), lax.optimization_barrier(jnp.sum(bias_terms, axis=0))[None, :]], axis=0)
        return (total + summed, jnp.concatenate([grad_q, grad_k, grad_v], axis=1))
    start = jnp.zeros((BLOCKS, D), jnp.float32)
    grads, qkv_grads = lax.scan(one_seq, start, (queries, keys, values, out_grad))
    grads_rows = grads.reshape(BLOCKS * DR, 128)
    off_rows = (block_offsets // 128).astype(jnp.int32)
    flat_rows = jnp.arange(FR).astype(jnp.int32)
    laid = lay_rows(grads_rows, off_rows, flat_rows, DR)
    bucket = laid.reshape(FLAT) * (1.0 / math.sqrt(TOKENS))
    return (bucket, qkv_grads)
```

```python
import math

import jax
import jax.numpy as jnp
from jax import lax
from jax.experimental import pallas as pl
from jax.experimental.pallas import tpu as pltpu
from jax.sharding import PartitionSpec as P

MESH = pl.DeviceIdType.MESH
BF = jnp.bfloat16
F32 = jnp.float32

HEAD = 128
TOK = 128
WIDTH = 12288
COLS = 768
PER = 96
NB = 80
B0 = 56
PAD = 56
GROWS = PAD + NB * PER + PAD
WIN = 50
CHUNK = 400
HALVES = ((0, 208), (208, 192))
OCH = 6
OW = WIDTH // OCH

CHAINS = ((-1, 0, 4), (1, 1, 4), (-1, 1, 3), (1, 0, 3))


def dot(a, b, ca, cb):
    return lax.dot_general(a, b, (((ca,), (cb,)), ((), ())), preferred_element_type=F32)


def kernel(q_hbm, k_hbm, v_hbm, o_hbm, w_hbm, off, bucket, qkv,
           O, W, G, F, S, R, At, q, K, V, probs, hg, gsend, grecv, send2, recv2, tab,
           lsem, ssem, rsem, s2send, s2recv):
    node = lax.axis_index("node")
    group = lax.axis_index("group")
    x, zlo = node // 4, node % 4
    y, zhi, k = group // 4, (group % 4) // 2, group % 2
    z = zhi * 4 + zlo

    def did(dx, dy, dz, dc):
        dx, dy, dz = lax.rem(dx + 8, 4), lax.rem(dy + 16, 8), lax.rem(dz + 16, 8)
        return (dx * 4 + lax.rem(dz, 4), dy * 4 + dz // 4 * 2 + dc)

    sib = did(x, y, z, 1 - k)
    nxt = (lax.rem(node + 1, 16), group)
    prv = (lax.rem(node + 15, 16), group)
    counter = [0]

    def send(src, dst, dev):
        i = counter[0]
        counter[0] += 1
        cp = pltpu.make_async_remote_copy(
            src_ref=src, dst_ref=dst, send_sem=ssem.at[i], recv_sem=rsem.at[i],
            device_id=dev, device_id_type=MESH)
        cp.start()
        sent.append(cp)
        return cp

    sent = []

    own_rows = pl.ds(pl.multiple_of(TOK * k, TOK), TOK)
    locals_ = [
        pltpu.make_async_copy(q_hbm.at[0], q, lsem.at[0]),
        pltpu.make_async_copy(k_hbm.at[0], K.at[pl.ds(TOK, TOK)], lsem.at[1]),
        pltpu.make_async_copy(v_hbm.at[0], V.at[pl.ds(TOK, TOK)], lsem.at[2]),
        pltpu.make_async_copy(o_hbm.at[0], O.at[own_rows], lsem.at[3]),
        pltpu.make_async_copy(w_hbm, W.at[node], lsem.at[4]),
    ]
    for c in locals_:
        c.start()

    bar = pltpu.get_barrier_semaphore()

    def sig(dev):
        pl.semaphore_signal(bar, inc=1, device_id=dev, device_id_type=MESH)

    near = [sib, nxt, prv, did(x, y + 1, z, k), did(x, y - 1, z, k), did(x, y, z + 1, k),
            did(x, y, z - 1, k), did(x + 1, y, z, k), did(x - 1, y, z, k)]
    for dev in near:
        sig(dev)
    src_core = x // 2
    odd = lax.rem(x, 2)
    mine = src_core == k

    def sig_far(i, carry):
        sx, r = i // 8, lax.rem(i, 8)
        sy = jnp.where(odd == 1, r, y)
        sz = jnp.where(odd == 1, z, r)

        @pl.when(jnp.logical_not(mine & (sx == x) & (sy == y) & (sz == z)))
        def _():
            sig(did(sx, sy, sz, src_core))
        return carry
    lax.fori_loop(0, 32, sig_far, 0)

    b0 = B0 * k

    def off_row(i):
        return lax.shift_right_logical(off[jnp.clip(i, 0, 128)], 7)

    def advance(i, f0):
        step = (i + 1 <= 128) & (off_row(i + 1) <= f0)
        return i + step.astype(jnp.int32)

    first = jnp.where(k == 0, -1, 61)
    flat0 = 6400 * k
    first = lax.fori_loop(0, 5, lambda _, i: advance(i, flat0), first)

    def table(w, i):
        f0 = flat0 + WIN * w
        i = advance(i, f0)
        a, b = off_row(i), off_row(i + 1)
        one = PAD + (i - b0) * PER + jnp.clip(f0 - a, 0, PER)
        two = PAD + (jnp.minimum(i + 1, 128) - b0) * PER + jnp.clip(f0 - b, -PAD, 0)
        tab[0, w] = jnp.clip(one, 0, GROWS - 56)
        tab[1, w] = jnp.clip(two, 0, GROWS - 56)
        tab[2, w] = jnp.where(i < 0, 0, a + PER - f0)
        tab[3, w] = jnp.where(i + 1 > 128, 2 * WIN, b - f0)
        return i
    lax.fori_loop(0, 128, table, first)

    rows8 = lax.broadcasted_iota(jnp.int32, (8, 2 * TOK), 0)
    At[pl.ds(HEAD, 8), :] = jnp.where(rows8 == 0, 1.0, 0.0)

    pl.semaphore_wait(bar, len(near) + 32 - mine.astype(jnp.int32))

    cp_k = send(k_hbm.at[0], K.at[pl.ds(0, TOK)], nxt)
    cp_v = send(v_hbm.at[0], V.at[pl.ds(0, TOK)], nxt)

    half = pl.multiple_of(64 * k, 64)

    def nbr(axis, delta):
        along_z = (k == 0) if axis == 0 else (k == 1)
        return did(x + jnp.where(along_z, 0, delta), y, z + jnp.where(along_z, delta, 0), k)

    def nid(a, b):
        dx, dz = jnp.where(k == 0, b, a), jnp.where(k == 0, a, b)
        return lax.rem(x + dx + 4, 4) * 4 + lax.rem(zlo + dz + 4, 4)

    def wpart(n, sub=None):
        if sub is None:
            return W.at[n, pl.ds(half, 64)]
        return W.at[n, pl.ds(half + 32 * sub, 32)]

    w_own = w_hbm.at[pl.ds(half, 64)]
    m1 = {d: send(w_own, wpart(node), nbr(0, d)) for d in (1, -1)}
    m2 = {}
    for d in (1, -1):
        m2[0, d] = send(w_own, wpart(node), nbr(1, d))
    cp_o = [send(o_hbm.at[0, :, pl.ds(OW * j, OW)], O.at[own_rows, pl.ds(OW * j, OW)], sib)
            for j in range(OCH)]

    f1, f2, wsib = {}, {}, []

    def stage1(d):
        m1[d].wait_recv()
        n = nid(-d, 0)
        f1[d] = send(wpart(n, 0 if d == 1 else 1), wpart(n, 0 if d == 1 else 1), nbr(0, d))
        for e in (1, -1):
            m2[-d, e] = send(wpart(n), wpart(n), nbr(1, e))
        wsib.append(send(wpart(n), wpart(n), sib))

    def stage1_far():
        for d in (1, -1):
            f1[d].wait_recv()
        n = nid(2, 0)
        for e in (1, -1):
            m2[2, e] = send(wpart(n), wpart(n), nbr(1, e))
        wsib.append(send(wpart(n), wpart(n), sib))

    def stage2(a):
        for e in (1, -1):
            m2[a, e].wait_recv()
            n = nid(a, -e)
            sub = 0 if e == 1 else 1
            f2[a, e] = send(wpart(n, sub), wpart(n, sub), nbr(1, e))
            wsib.append(send(wpart(n), wpart(n), sib))

    def stage2_far(a):
        for e in (1, -1):
            f2[a, e].wait_recv()
        n = nid(a, 2)
        wsib.append(send(wpart(n), wpart(n), sib))

    stage1(1)
    stage1(-1)

    for c in locals_[:3]:
        c.wait()
    cp_k.wait_recv()
    cp_v.wait_recv()
    scale = 1.0 / math.sqrt(HEAD)
    scores = dot(q[...], K[...], 1, 1) * scale
    rp = lax.broadcasted_iota(jnp.int32, (TOK, 2 * TOK), 0)
    cpos = lax.broadcasted_iota(jnp.int32, (TOK, 2 * TOK), 1)
    lowest = jnp.where(node == 0, TOK, 0)
    allowed = (cpos > rp) & (cpos <= rp + TOK) & (cpos >= lowest)
    scores = jnp.where(allowed, scores, -jnp.inf)
    top = jnp.max(scores, axis=1, keepdims=True)
    expo = jnp.exp(scores - top)
    pr = expo / jnp.sum(expo, axis=1, keepdims=True)
    probs[...] = pr
    att = dot(pr.astype(BF), V[...], 1, 0)
    att_cols = pl.ds(pl.multiple_of(TOK * k, TOK), TOK)
    At[pl.ds(0, HEAD), att_cols] = jnp.transpose(att)
    cp_a = send(At.at[pl.ds(0, HEAD), att_cols], At.at[pl.ds(0, HEAD), att_cols], sib)

    stage1_far()
    stage2(0)

    cp_a.wait_recv()
    locals_[3].wait()
    lhs = At[pl.ds(pl.multiple_of(b0, 8), NB), :].astype(BF)
    for j in range(OCH):
        cp_o[j].wait_recv()

        def mul(t, carry):
            prod = dot(lhs, O[:, pl.ds(pl.multiple_of(256 * t, 256), 256)], 1, 0)
            G[pl.ds(PAD + 2 * t, NB, stride=PER), :] = prod[:, :128]
            G[pl.ds(PAD + 2 * t + 1, NB, stride=PER), :] = prod[:, 128:]
            return carry
        lax.fori_loop(j * (OW // 256), (j + 1) * (OW // 256), mul, 0)

    rwin = lax.broadcasted_iota(jnp.int32, (56, 128), 0)

    def gather(delta):
        for a, p in ((0, y), (1, z)):
            d = lax.rem(p + delta + 16, 8)
            for m in range(8):
                if a == 0:
                    w = 16 * (m % 4) + 2 * d + m // 4
                else:
                    w = 64 + 16 * lax.rem(d, 4) + 2 * m + d // 4
                one = G[pl.ds(tab[0, w], 56), :]
                two = G[pl.ds(tab[1, w], 56), :]
                F[a, pl.ds(WIN * m, 56), :] = jnp.where(
                    rwin < tab[2, w], one, jnp.where(rwin >= tab[3, w], two, 0.0))
            S[a, d] = F[a, pl.ds(0, CHUNK), :].astype(BF)

    msgs = {}

    def ring(ch, s):
        direction, h, n = CHAINS[ch]
        lo, size = HALVES[h]
        rows = pl.ds(lo, size)
        for a, p in ((0, y), (1, z)):
            d = lax.rem(p + direction * (n - s) + 16, 8)
            if s > 0:
                msgs[a, ch, s - 1].wait_recv()
                S[a, d, rows] = (S[a, d, rows].astype(F32)
                                 + R[a, ch, s - 1, pl.ds(0, size)].astype(F32)).astype(BF)
            to = did(x, y + direction, z, k) if a == 0 else did(x, y, z + direction, k)
            msgs[a, ch, s] = send(S.at[a, d, rows], R.at[a, ch, s, pl.ds(0, size)], to)

    gather(4)
    ring(0, 0)
    ring(1, 0)
    gather(-3)
    ring(2, 0)
    gather(3)
    ring(3, 0)
    gather(-2)
    gather(2)
    for ch in range(4):
        ring(ch, 1)
    stage2(-1)
    stage2(1)
    stage2_far(0)
    gather(-1)
    gather(1)
    for ch in range(4):
        ring(ch, 2)
    gather(0)
    stage2(2)
    stage2_far(-1)
    stage2_far(1)
    for ch in range(2):
        ring(ch, 3)
    stage2_far(2)

    locals_[4].wait()
    for c in wsib:
        c.wait_recv()
    hg[...] = jnp.zeros((TOK, HEAD), F32)

    def head(n, carry):
        cols = pl.ds(pl.multiple_of(COLS * n, COLS), COLS)
        hg[...] += dot(O[own_rows, cols], W[n], 1, 1)
        return carry
    lax.fori_loop(0, 16, head, 0)
    head_low = hg[...].astype(BF)
    prob_grad = dot(head_low, V[...], 1, 1)
    pr = probs[...]
    center = jnp.sum(pr * prob_grad, axis=1, keepdims=True)
    sg = pr * (prob_grad - center) * scale
    grad_q = dot(sg.astype(BF), K[...], 1, 0)
    kg = dot(jnp.transpose(sg).astype(BF), q[...], 1, 0)
    vg = dot(jnp.transpose(pr).astype(BF), head_low, 1, 0)
    gsend[pl.ds(0, TOK), :] = kg[:TOK].astype(BF)
    gsend[pl.ds(TOK, TOK), :] = vg[:TOK].astype(BF)
    cp_g = send(gsend, grecv, prv)
    qkv[0, :, pl.ds(0, HEAD)] = grad_q.astype(BF)
    hg[...] = kg[TOK:]
    probs[:, pl.ds(0, HEAD)] = vg[TOK:]

    last = {0: (0, 3), 1: (3, 2), 2: (2, 2), 3: (1, 3)}
    for a, p in ((0, y), (1, z)):
        for h, (lo, size) in enumerate(HALVES):
            total = S[a, p, pl.ds(lo, size)].astype(F32)
            for ch, (direction, hh, n) in enumerate(CHAINS):
                if hh == h:
                    msgs[a, ch, n - 1].wait_recv()
                    total = total + R[a, ch, n - 1, pl.ds(0, size)].astype(F32)
            F[a, pl.ds(lo, size), :] = total
        for i in range(16):
            send2[16 * a + i] = F[a, pl.ds(25 * i, 32), :].astype(BF)

        def scatter(i, carry):
            r, dc = i // 2, lax.rem(i, 2)
            dx = 2 * k + a
            dy = y if a == 0 else r
            dz = r if a == 0 else z
            slot = x * 8 + (z if a == 0 else y)
            here = (dx == x) & (dy == y) & (dz == z) & (dc == k)

            @pl.when(here)
            def _():
                pltpu.make_async_copy(send2.at[16 * a + i], recv2.at[slot], s2recv).start()

            @pl.when(jnp.logical_not(here))
            def _():
                pltpu.make_async_remote_copy(
                    src_ref=send2.at[16 * a + i], dst_ref=recv2.at[slot],
                    send_sem=s2send, recv_sem=s2recv,
                    device_id=did(dx, dy, dz, dc), device_id_type=MESH).start()
            return carry
        lax.fori_loop(0, 16, scatter, 0)

    cp_g.wait_recv()
    qkv[0, :, pl.ds(HEAD, HEAD)] = (hg[...] + grecv[pl.ds(0, TOK), :].astype(F32)).astype(BF)
    qkv[0, :, pl.ds(2 * HEAD, HEAD)] = (
        probs[:, pl.ds(0, HEAD)] + grecv[pl.ds(TOK, TOK), :].astype(F32)).astype(BF)

    pltpu.make_async_remote_copy(
        src_ref=send2, dst_ref=recv2, send_sem=s2send, recv_sem=s2recv,
        device_id=sib, device_id_type=MESH).wait_recv()
    acc = recv2[0].astype(F32)
    for s in range(1, 32):
        acc = acc + recv2[s].astype(F32)
    bucket[...] = acc[:25] * (1.0 / math.sqrt(65536))

    for c in sent:
        c.wait_send()

    def drain(count):
        pltpu.make_async_remote_copy(
            src_ref=send2.at[pl.ds(0, count)], dst_ref=recv2.at[pl.ds(0, count)],
            send_sem=s2send, recv_sem=s2recv, device_id=sib, device_id_type=MESH).wait_send()

    @pl.when(mine)
    def _():
        drain(31)

    @pl.when(jnp.logical_not(mine))
    def _():
        drain(32)


def per_device(queries, keys, values, out_grad, out_weight, block_offsets):
    hbm = pl.BlockSpec(memory_space=pl.ANY)
    vmem = pl.BlockSpec(memory_space=pltpu.VMEM)
    messages = 96
    bucket, qkv = pl.pallas_call(
        kernel,
        out_shape=(jax.ShapeDtypeStruct((25, 128), F32), jax.ShapeDtypeStruct((1, TOK, 3 * HEAD), BF)),
        in_specs=[hbm] * 5 + [pl.BlockSpec(memory_space=pltpu.SMEM)],
        out_specs=(vmem, vmem),
        scratch_shapes=[
            pltpu.VMEM((2 * TOK, WIDTH), BF),
            pltpu.VMEM((16, HEAD, COLS), BF),
            pltpu.VMEM((GROWS, 128), F32),
            pltpu.VMEM((2, 408, 128), F32),
            pltpu.VMEM((2, 8, CHUNK, 128), BF),
            pltpu.VMEM((2, 4, 4, 208, 128), BF),
            pltpu.VMEM((HEAD + 8, 2 * TOK), F32),
            pltpu.VMEM((TOK, HEAD), BF),
            pltpu.VMEM((2 * TOK, HEAD), BF),
            pltpu.VMEM((2 * TOK, HEAD), BF),
            pltpu.VMEM((TOK, 2 * TOK), F32),
            pltpu.VMEM((TOK, HEAD), F32),
            pltpu.VMEM((2 * TOK, HEAD), BF),
            pltpu.VMEM((2 * TOK, HEAD), BF),
            pltpu.VMEM((32, 32, 128), BF),
            pltpu.VMEM((32, 32, 128), BF),
            pltpu.SMEM((4, 128), jnp.int32),
            pltpu.SemaphoreType.DMA((5,)),
            pltpu.SemaphoreType.DMA((messages,)),
            pltpu.SemaphoreType.DMA((messages,)),
            pltpu.SemaphoreType.DMA,
            pltpu.SemaphoreType.DMA,
        ],
        compiler_params=pltpu.CompilerParams(
            collective_id=0, has_side_effects=True, vmem_limit_bytes=40 << 20),
        name="attention_backward",
    )(queries, keys, values, out_grad, out_weight, block_offsets)
    return bucket.reshape(3200), qkv


def solution(mesh):
    return jax.shard_map(
        per_device,
        mesh=mesh,
        in_specs=(
            P("group", "node", None),
            P("group", "node", None),
            P("group", "node", None),
            P("group", "node", None),
            P(None, "node"),
            P(),
        ),
        out_specs=(P(("node", "group")), P("group", "node", None)),
        check_vma=False,
    )
```

```python
import math

import jax
import jax.numpy as jnp
from jax import lax
from jax.experimental import pallas as pl
from jax.experimental.pallas import tpu as pltpu
from jax.sharding import PartitionSpec as P

MESH = pl.DeviceIdType.MESH
BF = jnp.bfloat16
F32 = jnp.float32

HEAD = 128
TOK = 128
WIDTH = 12288
COLS = 768
PER = 96
NB = 80
B0 = 56
PAD = 56
STEP = 97
GROWS = PAD + NB * STEP + PAD
WIN = 50
CHUNK = 400
HALVES = ((0, 208), (208, 192))
OCH = 6
OW = WIDTH // OCH

CHAINS = ((-1, 0, 4), (1, 1, 4), (-1, 1, 3), (1, 0, 3))


def dot(a, b, ca, cb):
    return lax.dot_general(a, b, (((ca,), (cb,)), ((), ())), preferred_element_type=F32)


def kernel(q_hbm, k_hbm, v_hbm, o_hbm, w_hbm, off_hbm, bucket, qkv,
           O, W, G, F, S, R, At, q, K, V, probs, hg, gsend, grecv, send2, recv2, off, tab,
           lsem, ssem, rsem, s2send, s2recv):
    node = lax.axis_index("node")
    group = lax.axis_index("group")
    x, zlo = node // 4, node % 4
    y, zhi, k = group // 4, (group % 4) // 2, group % 2
    z = zhi * 4 + zlo

    def did(dx, dy, dz, dc):
        dx, dy, dz = lax.rem(dx + 8, 4), lax.rem(dy + 16, 8), lax.rem(dz + 16, 8)
        return (dx * 4 + lax.rem(dz, 4), dy * 4 + dz // 4 * 2 + dc)

    sib = did(x, y, z, 1 - k)
    nxt = (lax.rem(node + 1, 16), group)
    prv = (lax.rem(node + 15, 16), group)
    counter = [0]

    def send(src, dst, dev):
        i = counter[0]
        counter[0] += 1
        cp = pltpu.make_async_remote_copy(
            src_ref=src, dst_ref=dst, send_sem=ssem.at[i], recv_sem=rsem.at[i],
            device_id=dev, device_id_type=MESH)
        cp.start()
        sent.append(cp)
        return cp

    sent = []

    bar = pltpu.get_barrier_semaphore()
    chip_line = [did(x + dx, y, z, dc) for dx in range(4) for dc in (k, 1 - k)][1:]
    near = [prv, did(x, y + 1, z, k), did(x, y - 1, z, k), did(x, y, z + 1, k), did(x, y, z - 1, k)] + chip_line
    for dev in near:
        pl.semaphore_signal(bar, inc=1, device_id=dev, device_id_type=MESH)
    src_core = x // 2
    mine = src_core == k

    own_rows = pl.ds(pl.multiple_of(TOK * k, TOK), TOK)
    locals_ = [
        pltpu.make_async_copy(q_hbm.at[0], q, lsem.at[0]),
        pltpu.make_async_copy(k_hbm.at[0], K.at[pl.ds(TOK, TOK)], lsem.at[1]),
        pltpu.make_async_copy(v_hbm.at[0], V.at[pl.ds(TOK, TOK)], lsem.at[2]),
        pltpu.make_async_copy(o_hbm.at[0], O.at[own_rows], lsem.at[3]),
        pltpu.make_async_copy(w_hbm, W.at[node], lsem.at[4]),
        pltpu.make_async_copy(off_hbm, off, lsem.at[5]),
    ]
    for c in locals_:
        c.start()

    rows8 = lax.broadcasted_iota(jnp.int32, (8, 2 * TOK), 0)
    At[pl.ds(HEAD, 8), :] = jnp.where(rows8 == 0, 1.0, 0.0)

    pl.semaphore_wait(bar, len(near))

    cp_k = send(k_hbm.at[0], K.at[pl.ds(0, TOK)], nxt)
    cp_v = send(v_hbm.at[0], V.at[pl.ds(0, TOK)], nxt)

    half = pl.multiple_of(64 * k, 64)

    def nbr(axis, delta):
        along_z = (k == 0) if axis == 0 else (k == 1)
        return did(x + jnp.where(along_z, 0, delta), y, z + jnp.where(along_z, delta, 0), k)

    def nid(a, b):
        dx, dz = jnp.where(k == 0, b, a), jnp.where(k == 0, a, b)
        return lax.rem(x + dx + 4, 4) * 4 + lax.rem(zlo + dz + 4, 4)

    def wpart(n, sub=None):
        if sub is None:
            return W.at[n, pl.ds(half, 64)]
        return W.at[n, pl.ds(half + 32 * sub, 32)]

    w_own = w_hbm.at[pl.ds(half, 64)]
    m1 = {d: send(w_own, wpart(node), nbr(0, d)) for d in (1, -1)}
    m2 = {}
    for d in (1, -1):
        m2[0, d] = send(w_own, wpart(node), nbr(1, d))
    cp_o = [send(o_hbm.at[0, :, pl.ds(OW * j, OW)], O.at[own_rows, pl.ds(OW * j, OW)], sib)
            for j in range(OCH)]

    f1, f2, wsib = {}, {}, {}

    def stage1(d):
        m1[d].wait_recv()
        n = nid(-d, 0)
        f1[d] = send(wpart(n, 0 if d == 1 else 1), wpart(n, 0 if d == 1 else 1), nbr(0, d))
        for e in (1, -1):
            m2[-d, e] = send(wpart(n), wpart(n), nbr(1, e))
        wsib[-d, 0] = send(wpart(n), wpart(n), sib)

    def stage1_far():
        for d in (1, -1):
            f1[d].wait_recv()
        n = nid(2, 0)
        for e in (1, -1):
            m2[2, e] = send(wpart(n), wpart(n), nbr(1, e))
        wsib[2, 0] = send(wpart(n), wpart(n), sib)

    def stage2(a):
        for e in (1, -1):
            m2[a, e].wait_recv()
            n = nid(a, -e)
            sub = 0 if e == 1 else 1
            f2[a, e] = send(wpart(n, sub), wpart(n, sub), nbr(1, e))
            wsib[a, -e] = send(wpart(n), wpart(n), sib)

    def stage2_far(a):
        for e in (1, -1):
            f2[a, e].wait_recv()
        n = nid(a, 2)
        wsib[a, 2] = send(wpart(n), wpart(n), sib)

    b0 = B0 * k
    locals_[5].wait()

    def off_row(i):
        return lax.shift_right_logical(off[jnp.clip(i, 0, 128)], 7)

    def advance(i, f0):
        step = (i + 1 <= 128) & (off_row(i + 1) <= f0)
        return i + step.astype(jnp.int32)

    first = jnp.where(k == 0, -1, 61)
    flat0 = 6400 * k
    first = lax.fori_loop(0, 5, lambda _, i: advance(i, flat0), first)

    def table(w, i):
        f0 = flat0 + WIN * w
        i = advance(i, f0)
        a, b = off_row(i), off_row(i + 1)
        one = PAD + (i - b0) * STEP + jnp.clip(f0 - a, 0, PER)
        two = PAD + (jnp.minimum(i + 1, 128) - b0) * STEP + jnp.clip(f0 - b, -PAD, 0)
        tab[0, w] = jnp.clip(one, 0, GROWS - 56)
        tab[1, w] = jnp.clip(two, 0, GROWS - 56)
        tab[2, w] = jnp.where(i < 0, 0, a + PER - f0)
        tab[3, w] = jnp.where(i + 1 > 128, 2 * WIN, b - f0)
        return i
    lax.fori_loop(0, 128, table, first)

    for c in locals_[:3]:
        c.wait()
    cp_k.wait_recv()
    cp_v.wait_recv()
    scale = 1.0 / math.sqrt(HEAD)
    scores = dot(q[...], K[...], 1, 1) * scale
    rp = lax.broadcasted_iota(jnp.int32, (TOK, 2 * TOK), 0)
    cpos = lax.broadcasted_iota(jnp.int32, (TOK, 2 * TOK), 1)
    lowest = jnp.where(node == 0, TOK, 0)
    allowed = (cpos > rp) & (cpos <= rp + TOK) & (cpos >= lowest)
    scores = jnp.where(allowed, scores, -jnp.inf)
    top = jnp.max(scores, axis=1, keepdims=True)
    expo = jnp.exp(scores - top)
    pr = expo / jnp.sum(expo, axis=1, keepdims=True)
    probs[...] = pr
    att = dot(pr.astype(BF), V[...], 1, 0)
    att_cols = pl.ds(pl.multiple_of(TOK * k, TOK), TOK)
    At[pl.ds(0, HEAD), att_cols] = jnp.transpose(att)
    cp_a = send(At.at[pl.ds(0, HEAD), att_cols], At.at[pl.ds(0, HEAD), att_cols], sib)

    stage1(1)
    stage1(-1)

    cp_a.wait_recv()
    locals_[3].wait()
    lhs = At[pl.ds(pl.multiple_of(b0, 8), NB), :].astype(BF)

    def mul(t, carry):
        prod = dot(lhs, O[:, pl.ds(pl.multiple_of(256 * t, 256), 256)], 1, 0)
        G[pl.ds(PAD + 2 * t, NB, stride=STEP), :] = prod[:, :128]
        G[pl.ds(PAD + 2 * t + 1, NB, stride=STEP), :] = prod[:, 128:]
        return carry

    def muls(j):
        cp_o[j].wait_recv()
        lax.fori_loop(j * (OW // 256), (j + 1) * (OW // 256), mul, 0, unroll=2)

    muls(0)
    muls(1)
    stage1_far()
    muls(2)
    muls(3)
    stage2(0)
    muls(4)
    muls(5)

    rwin = lax.broadcasted_iota(jnp.int32, (56, 128), 0)

    def gather(delta):
        for a, p in ((0, y), (1, z)):
            d = lax.rem(p + delta + 16, 8)
            for m in range(8):
                if a == 0:
                    w = 16 * (m % 4) + 2 * d + m // 4
                else:
                    w = 64 + 16 * lax.rem(d, 4) + 2 * m + d // 4
                one = G[pl.ds(tab[0, w], 56), :]
                two = G[pl.ds(tab[1, w], 56), :]
                F[a, pl.ds(WIN * m, 56), :] = jnp.where(
                    rwin < tab[2, w], one, jnp.where(rwin >= tab[3, w], two, 0.0))
            S[a, d] = F[a, pl.ds(0, CHUNK), :].astype(BF)

    msgs = {}

    def ring(ch, s):
        direction, h, n = CHAINS[ch]
        lo, size = HALVES[h]
        rows = pl.ds(lo, size)
        for a, p in ((0, y), (1, z)):
            d = lax.rem(p + direction * (n - s) + 16, 8)
            if s > 0:
                msgs[a, ch, s - 1].wait_recv()
                S[a, d, rows] = (S[a, d, rows].astype(F32)
                                 + R[a, ch, s - 1, pl.ds(0, size)].astype(F32)).astype(BF)
            to = did(x, y + direction, z, k) if a == 0 else did(x, y, z + direction, k)
            msgs[a, ch, s] = send(S.at[a, d, rows], R.at[a, ch, s, pl.ds(0, size)], to)

    gather(4)
    ring(0, 0)
    ring(1, 0)
    gather(-3)
    ring(2, 0)
    gather(3)
    ring(3, 0)
    gather(-2)
    gather(2)
    gather(-1)
    gather(1)
    gather(0)

    hg[...] = jnp.zeros((TOK, HEAD), F32)
    locals_[4].wait()

    def head(keys, shards):
        for key in keys:
            wsib[key].wait_recv()
        total = hg[...]
        for dx, dz in shards:
            n = lax.rem(x + dx + 4, 4) * 4 + lax.rem(zlo + dz + 4, 4)
            cols = pl.ds(pl.multiple_of(COLS * n, COLS), COLS)
            total = total + dot(O[own_rows, cols], W[n], 1, 1)
        hg[...] = total

    head([(1, 0), (-1, 0), (0, 1), (0, -1)], [(0, 0), (1, 0), (-1, 0), (0, 1), (0, -1)])
    stage2(-1)
    stage2(1)
    for ch in range(4):
        ring(ch, 1)
    head([(1, 1), (-1, 1), (1, -1), (-1, -1)], [(1, 1), (-1, 1), (1, -1), (-1, -1)])
    stage2_far(0)
    stage2(2)
    for ch in range(4):
        ring(ch, 2)
    stage2_far(-1)
    stage2_far(1)
    head([(2, 0), (0, 2)], [(2, 0), (0, 2)])
    stage2_far(2)
    for ch in range(2):
        ring(ch, 3)
    head([(2, 1), (2, -1), (-1, 2), (1, 2), (2, 2)], [(2, 1), (2, -1), (1, 2), (-1, 2), (2, 2)])

    head_low = hg[...].astype(BF)
    prob_grad = dot(head_low, V[...], 1, 1)
    pr = probs[...]
    center = jnp.sum(pr * prob_grad, axis=1, keepdims=True)
    sg = pr * (prob_grad - center) * scale
    grad_q = dot(sg.astype(BF), K[...], 1, 0)
    kg = dot(jnp.transpose(sg).astype(BF), q[...], 1, 0)
    vg = dot(jnp.transpose(pr).astype(BF), head_low, 1, 0)
    gsend[pl.ds(0, TOK), :] = kg[:TOK].astype(BF)
    gsend[pl.ds(TOK, TOK), :] = vg[:TOK].astype(BF)
    cp_g = send(gsend, grecv, prv)
    qkv[0, :, pl.ds(0, HEAD)] = grad_q.astype(BF)
    hg[...] = kg[TOK:]
    probs[:, pl.ds(0, HEAD)] = vg[TOK:]

    for a, p in ((0, y), (1, z)):
        for h, (lo, size) in enumerate(HALVES):
            total = S[a, p, pl.ds(lo, size)].astype(F32)
            for ch, (direction, hh, n) in enumerate(CHAINS):
                if hh == h:
                    msgs[a, ch, n - 1].wait_recv()
                    total = total + R[a, ch, n - 1, pl.ds(0, size)].astype(F32)
            F[a, pl.ds(lo, size), :] = total
        for i in range(16):
            send2[16 * a + i] = F[a, pl.ds(25 * i, 32), :].astype(BF)

    for a in range(2):
        def scatter(i, carry):
            r, dc = i // 2, lax.rem(i, 2)
            dx = 2 * k + a
            dy = y if a == 0 else r
            dz = r if a == 0 else z
            slot = x * 8 + (z if a == 0 else y)
            here = (dx == x) & (dy == y) & (dz == z) & (dc == k)

            @pl.when(here)
            def _():
                pltpu.make_async_copy(send2.at[16 * a + i], recv2.at[slot], s2recv).start()

            @pl.when(jnp.logical_not(here))
            def _():
                pltpu.make_async_remote_copy(
                    src_ref=send2.at[16 * a + i], dst_ref=recv2.at[slot],
                    send_sem=s2send, recv_sem=s2recv,
                    device_id=did(dx, dy, dz, dc), device_id_type=MESH).start()
            return carry
        lax.fori_loop(0, 16, scatter, 0)

    cp_g.wait_recv()
    qkv[0, :, pl.ds(HEAD, HEAD)] = (hg[...] + grecv[pl.ds(0, TOK), :].astype(F32)).astype(BF)
    qkv[0, :, pl.ds(2 * HEAD, HEAD)] = (
        probs[:, pl.ds(0, HEAD)] + grecv[pl.ds(TOK, TOK), :].astype(F32)).astype(BF)

    pltpu.make_async_remote_copy(
        src_ref=send2, dst_ref=recv2, send_sem=s2send, recv_sem=s2recv,
        device_id=sib, device_id_type=MESH).wait_recv()
    acc = recv2[0].astype(F32)
    for s in range(1, 32):
        acc = acc + recv2[s].astype(F32)
    bucket[...] = acc[:25] * (1.0 / math.sqrt(65536))

    for c in sent:
        c.wait_send()

    def drain(count):
        pltpu.make_async_remote_copy(
            src_ref=send2.at[pl.ds(0, count)], dst_ref=recv2.at[pl.ds(0, count)],
            send_sem=s2send, recv_sem=s2recv, device_id=sib, device_id_type=MESH).wait_send()

    @pl.when(mine)
    def _():
        drain(31)

    @pl.when(jnp.logical_not(mine))
    def _():
        drain(32)


def per_device(queries, keys, values, out_grad, out_weight, block_offsets):
    hbm = pl.BlockSpec(memory_space=pltpu.HBM)
    vmem = pl.BlockSpec(memory_space=pltpu.VMEM)
    messages = 96
    bucket, qkv = pl.pallas_call(
        kernel,
        out_shape=(jax.ShapeDtypeStruct((25, 128), F32), jax.ShapeDtypeStruct((1, TOK, 3 * HEAD), BF)),
        in_specs=[hbm] * 6,
        out_specs=(vmem, vmem),
        scratch_shapes=[
            pltpu.VMEM((2 * TOK, WIDTH), BF),
            pltpu.VMEM((16, HEAD, COLS), BF),
            pltpu.VMEM((GROWS, 128), F32),
            pltpu.VMEM((2, 408, 128), F32),
            pltpu.VMEM((2, 8, CHUNK, 128), BF),
            pltpu.VMEM((2, 4, 4, 208, 128), BF),
            pltpu.VMEM((HEAD + 8, 2 * TOK), F32),
            pltpu.VMEM((TOK, HEAD), BF),
            pltpu.VMEM((2 * TOK, HEAD), BF),
            pltpu.VMEM((2 * TOK, HEAD), BF),
            pltpu.VMEM((TOK, 2 * TOK), F32),
            pltpu.VMEM((TOK, HEAD), F32),
            pltpu.VMEM((2 * TOK, HEAD), BF),
            pltpu.VMEM((2 * TOK, HEAD), BF),
            pltpu.VMEM((32, 32, 128), BF),
            pltpu.VMEM((32, 32, 128), BF),
            pltpu.SMEM((129,), jnp.int32),
            pltpu.SMEM((4, 128), jnp.int32),
            pltpu.SemaphoreType.DMA((6,)),
            pltpu.SemaphoreType.DMA((messages,)),
            pltpu.SemaphoreType.DMA((messages,)),
            pltpu.SemaphoreType.DMA,
            pltpu.SemaphoreType.DMA,
        ],
        compiler_params=pltpu.CompilerParams(
            collective_id=0, has_side_effects=True, vmem_limit_bytes=60 << 20),
        name="attention_backward",
    )(queries, keys, values, out_grad, out_weight, block_offsets)
    return bucket.reshape(3200), qkv


def solution(mesh):
    return jax.shard_map(
        per_device,
        mesh=mesh,
        in_specs=(
            P("group", "node", None),
            P("group", "node", None),
            P("group", "node", None),
            P("group", "node", None),
            P(None, "node"),
            P(),
        ),
        out_specs=(P(("node", "group")), P("group", "node", None)),
        check_vma=False,
    )
```

```python
import math

import jax
import jax.numpy as jnp
from jax import lax
from jax.experimental import pallas as pl
from jax.experimental.pallas import tpu as pltpu
from jax.sharding import PartitionSpec as P

MESH = pl.DeviceIdType.MESH
BF = jnp.bfloat16
F32 = jnp.float32

HEAD = 128
TOK = 128
WIDTH = 12288
COLS = 768
PER = 96
NB = 80
B0 = 56
PAD = 56
STEP = 97
GROWS = PAD + NB * STEP + PAD
WIN = 50
CHUNK = 400
HALVES = ((0, 208), (208, 192))
OCH = 6
OW = WIDTH // OCH

STEPS = ((-4, -2), (-3, -1), (3, 1), (-1, -1), (1, 1), (-2, -2), (2, 2))


def dot(a, b, ca, cb):
    return lax.dot_general(a, b, (((ca,), (cb,)), ((), ())), preferred_element_type=F32)


def kernel(q_hbm, k_hbm, v_hbm, o_hbm, w_hbm, off_hbm, bucket, qkv,
           O, W, G, F, S, R, At, q, K, V, probs, hg, gsend, grecv, send2, recv2, off, first, tab,
           lsem, ssem, rsem, s2send, s2recv):
    node = lax.axis_index("node")
    group = lax.axis_index("group")
    x, zlo = node // 4, node % 4
    y, zhi, k = group // 4, (group % 4) // 2, group % 2
    z = zhi * 4 + zlo

    def did(dx, dy, dz, dc):
        dx, dy, dz = (dx + 8) & 3, (dy + 16) & 7, (dz + 16) & 7
        return (dx * 4 + (dz & 3), dy * 4 + (dz >> 2) * 2 + dc)

    sib = did(x, y, z, 1 - k)
    nxt = (lax.rem(node + 1, 16), group)
    prv = (lax.rem(node + 15, 16), group)
    counter = [0]

    def send(src, dst, dev):
        i = counter[0]
        counter[0] += 1
        cp = pltpu.make_async_remote_copy(
            src_ref=src, dst_ref=dst, send_sem=ssem.at[i], recv_sem=rsem.at[i],
            device_id=dev, device_id_type=MESH)
        cp.start()
        sent.append(cp)
        return cp

    sent = []

    bar = pltpu.get_barrier_semaphore()
    chip_line = [did(x + dx, y, z, dc) for dx in range(4) for dc in (k, 1 - k)][1:]
    near = [prv] + [did(x, y + d, z, k) for d in (1, -1, 2, -2)] + [did(x, y, z + d, k) for d in (1, -1, 2, -2)] + chip_line
    for dev in near:
        pl.semaphore_signal(bar, inc=1, device_id=dev, device_id_type=MESH)
    src_core = x // 2
    mine = src_core == k

    own_rows = pl.ds(pl.multiple_of(TOK * k, TOK), TOK)
    locals_ = [
        pltpu.make_async_copy(q_hbm.at[0], q, lsem.at[0]),
        pltpu.make_async_copy(k_hbm.at[0], K.at[pl.ds(TOK, TOK)], lsem.at[1]),
        pltpu.make_async_copy(v_hbm.at[0], V.at[pl.ds(TOK, TOK)], lsem.at[2]),
        pltpu.make_async_copy(o_hbm.at[0], O.at[own_rows], lsem.at[3]),
        pltpu.make_async_copy(w_hbm, W.at[node], lsem.at[4]),
        pltpu.make_async_copy(off_hbm, off, lsem.at[5]),
    ]
    for c in locals_:
        c.start()

    rows8 = lax.broadcasted_iota(jnp.int32, (8, 2 * TOK), 0)
    At[pl.ds(HEAD, 8), :] = jnp.where(rows8 == 0, 1.0, 0.0)

    pl.semaphore_wait(bar, len(near))

    cp_k = send(k_hbm.at[0], K.at[pl.ds(0, TOK)], nxt)
    cp_v = send(v_hbm.at[0], V.at[pl.ds(0, TOK)], nxt)

    half = pl.multiple_of(64 * k, 64)

    def nbr(axis, delta):
        along_z = (k == 0) if axis == 0 else (k == 1)
        return did(x + jnp.where(along_z, 0, delta), y, z + jnp.where(along_z, delta, 0), k)

    def nid(a, b):
        dx, dz = jnp.where(k == 0, b, a), jnp.where(k == 0, a, b)
        return lax.rem(x + dx + 4, 4) * 4 + lax.rem(zlo + dz + 4, 4)

    def wpart(n):
        return W.at[n, pl.ds(half, 64)]

    def relay(n, e):
        part = W.at[n, pl.ds(half + (0 if e == 1 else 32), 32)]
        return send(part, part, nbr(relay_axis[0], e))

    relay_axis = [0]

    def spread(a, src):
        for e in (1, -1):
            m2[a, e] = send(src, wpart(nid(a, 0)), nbr(1, e))

    def share(a, b):
        wsib[a, b] = send(wpart(nid(a, b)), wpart(nid(a, b)), sib)

    def first_near():
        relay_axis[0] = 0
        for e in (1, -1):
            m1[e].wait_recv()
            f1[e] = relay(nid(-e, 0), e)
        for a in (-1, 1):
            spread(a, wpart(nid(a, 0)))
            share(a, 0)

    def first_far():
        for e in (1, -1):
            f1[e].wait_recv()
        spread(2, wpart(nid(2, 0)))
        share(2, 0)

    def second_near(a):
        relay_axis[0] = 1
        for e in (1, -1):
            m2[a, e].wait_recv()
            f2[a, e] = relay(nid(a, -e), e)
        for b in (-1, 1):
            share(a, b)

    def second_far(a):
        for e in (1, -1):
            f2[a, e].wait_recv()
        share(a, 2)

    w_own = w_hbm.at[pl.ds(half, 64)]
    m1, m2, f1, f2, wsib = {}, {}, {}, {}, {}
    for e in (1, -1):
        m1[e] = send(w_own, wpart(node), nbr(0, e))
    spread(0, w_own)
    cp_o = [send(o_hbm.at[0, :, pl.ds(OW * j, OW)], O.at[own_rows, pl.ds(OW * j, OW)], sib)
            for j in range(OCH)]

    b0 = B0 * k
    locals_[5].wait()
    for i in range(8):
        first[i] = -100000
        first[137 + i] = 100000

    def rows_of(i, carry):
        first[8 + i] = lax.shift_right_logical(off[i], 7)
        return carry
    lax.fori_loop(0, 129, rows_of, 0, unroll=43)

    def table(w):
        f0 = 6400 * k + WIN * w
        low = lax.shift_right_logical((f0 - 416 + 8 * PER) * 43691, 22)
        at = low
        for j in range(1, 6):
            at = at + (first[low + j] <= f0).astype(jnp.int32)
        a, b = first[at] - f0, first[at + 1] - f0
        base = PAD + (at - 8 - b0) * STEP
        tab[0, w] = base + jnp.minimum(-a, PER)
        tab[1, w] = base + STEP - jnp.clip(b, 0, PAD)
        tab[2, w] = a + PER
        tab[3, w] = b

    for c in locals_[:3]:
        c.wait()
    cp_k.wait_recv()
    cp_v.wait_recv()
    scale = 1.0 / math.sqrt(HEAD)
    scores = dot(q[...], K[...], 1, 1) * scale
    rp = lax.broadcasted_iota(jnp.int32, (TOK, 2 * TOK), 0)
    cpos = lax.broadcasted_iota(jnp.int32, (TOK, 2 * TOK), 1)
    lowest = jnp.where(node == 0, TOK, 0)
    allowed = (cpos > rp) & (cpos <= rp + TOK) & (cpos >= lowest)
    scores = jnp.where(allowed, scores, -jnp.inf)
    top = jnp.max(scores, axis=1, keepdims=True)
    expo = jnp.exp(scores - top)
    pr = expo / jnp.sum(expo, axis=1, keepdims=True)
    probs[...] = pr
    att = dot(pr.astype(BF), V[...], 1, 0)
    att_cols = pl.ds(pl.multiple_of(TOK * k, TOK), TOK)
    At[pl.ds(0, HEAD), att_cols] = jnp.transpose(att)
    cp_a = send(At.at[pl.ds(0, HEAD), att_cols], At.at[pl.ds(0, HEAD), att_cols], sib)
    first_near()

    cp_a.wait_recv()
    locals_[3].wait()
    lhs = At[pl.ds(pl.multiple_of(b0, 8), NB), :].astype(BF)

    for t in range(WIDTH // 256):
        if t % (OW // 256) == 0:
            cp_o[t // (OW // 256)].wait_recv()
        prod = dot(lhs, O[:, pl.ds(256 * t, 256)], 1, 0)
        G[pl.ds(PAD + 2 * t, NB, stride=STEP), :] = prod[:, :128]
        G[pl.ds(PAD + 2 * t + 1, NB, stride=STEP), :] = prod[:, 128:]
        for w in range(128 * t // 48, 128 * (t + 1) // 48):
            table(w)

    rwin = lax.broadcasted_iota(jnp.int32, (56, 128), 0)

    def gather(delta):
        for a, p in ((0, y), (1, z)):
            d = (p + delta + 16) & 7
            for m in range(8):
                if a == 0:
                    w = 16 * (m % 4) + 2 * d + m // 4
                else:
                    w = 64 + 16 * (d & 3) + 2 * m + (d >> 2)
                one = G[pl.ds(tab[0, w], 56), :]
                two = G[pl.ds(tab[1, w], 56), :]
                F[a, pl.ds(WIN * m, 56), :] = jnp.where(
                    rwin < tab[2, w], one, jnp.where(rwin >= tab[3, w], two, 0.0))
            S[a, d] = F[a, pl.ds(0, CHUNK), :].astype(BF)

    msgs = {}

    def ring(h, m, parts=()):
        lo, size = HALVES[h]
        sign = 1 - 2 * h
        owner, target = STEPS[m]
        rows = pl.ds(lo, size)
        for a, p in ((0, y), (1, z)):
            d = (p + sign * owner + 16) & 7
            if parts:
                total = S[a, d, rows].astype(F32)
                for i in parts:
                    msgs[a, h, i].wait_recv()
                    total = total + R[a, h, i, pl.ds(0, size)].astype(F32)
                S[a, d, rows] = total.astype(BF)
            t = sign * target
            to = did(x, y + t, z, k) if a == 0 else did(x, y, z + t, k)
            msgs[a, h, m] = send(S.at[a, d, rows], R.at[a, h, m, pl.ds(0, size)], to)

    for delta in (4, -3, 3):
        gather(delta)
    for m in (0, 1, 2):
        ring(0, m)
    for delta in (-1, 1, -2, 2, 0):
        gather(delta)
    for m in (0, 1, 2):
        ring(1, m)
    second_near(0)
    first_far()
    for m in (3, 4):
        ring(0, m)
        ring(1, m)
    second_near(-1)
    second_near(1)
    hg[...] = jnp.zeros((TOK, HEAD), F32)
    locals_[4].wait()

    def head(keys, shards):
        for key in keys:
            wsib[key].wait_recv()
        total = hg[...]
        for dx, dz in shards:
            n = ((x + dx + 4) & 3) * 4 + ((zlo + dz + 4) & 3)
            cols = pl.ds(pl.multiple_of(COLS * n, COLS), COLS)
            total = total + dot(O[own_rows, cols], W[n], 1, 1)
        hg[...] = total

    for h in (0, 1):
        ring(h, 5, (0, 1))
        ring(h, 6, (2,))
    second_near(2)
    second_far(0)
    head([(1, 0), (-1, 0), (2, 0), (0, 1), (0, -1), (0, 2)],
         [(0, 0), (1, 0), (-1, 0), (2, 0), (0, 1), (0, -1), (0, 2)])
    head([(1, 1), (-1, 1), (1, -1), (-1, -1)], [(1, 1), (-1, 1), (1, -1), (-1, -1)])
    second_far(-1)
    second_far(1)

    for h, (lo, size) in enumerate(HALVES):
        for a, p in ((0, y), (1, z)):
            total = S[a, p, pl.ds(lo, size)].astype(F32)
            for i in (3, 4, 5, 6):
                msgs[a, h, i].wait_recv()
                total = total + R[a, h, i, pl.ds(0, size)].astype(F32)
            F[a, pl.ds(lo, size), :] = total
            for i in range(8 * h, 8 * h + 8):
                send2[16 * a + i] = F[a, pl.ds(25 * i, 32), :].astype(BF)
        for i in range(8 * h, 8 * h + 8):
            r, dc = i // 2, i % 2
            for a, p in ((0, z), (1, y)):
                src, dst = send2.at[16 * a + i], recv2.at[x * 8 + p]
                to = did(2 * k + a, y, r, dc) if a == 0 else did(2 * k + a, r, z, dc)
                here = (2 * k + a == x) & (p == r) & (k == dc)

                @pl.when(jnp.logical_not(here))
                def _():
                    pltpu.make_async_remote_copy(
                        src_ref=src, dst_ref=dst, send_sem=s2send, recv_sem=s2recv,
                        device_id=to, device_id_type=MESH).start()

                @pl.when(here)
                def _():
                    pltpu.make_async_copy(src, dst, s2recv).start()

    second_far(2)
    head([(2, 1), (2, -1), (-1, 2), (1, 2), (2, 2)], [(2, 1), (2, -1), (1, 2), (-1, 2), (2, 2)])

    head_low = hg[...].astype(BF)
    prob_grad = dot(head_low, V[...], 1, 1)
    pr = probs[...]
    center = jnp.sum(pr * prob_grad, axis=1, keepdims=True)
    sg = pr * (prob_grad - center) * scale
    grad_q = dot(sg.astype(BF), K[...], 1, 0)
    kg = dot(jnp.transpose(sg).astype(BF), q[...], 1, 0)
    vg = dot(jnp.transpose(pr).astype(BF), head_low, 1, 0)
    gsend[pl.ds(0, TOK), :] = kg[:TOK].astype(BF)
    gsend[pl.ds(TOK, TOK), :] = vg[:TOK].astype(BF)
    cp_g = send(gsend, grecv, prv)
    qkv[0, :, pl.ds(0, HEAD)] = grad_q.astype(BF)
    hg[...] = kg[TOK:]
    probs[:, pl.ds(0, HEAD)] = vg[TOK:]


    cp_g.wait_recv()
    qkv[0, :, pl.ds(HEAD, HEAD)] = (hg[...] + grecv[pl.ds(0, TOK), :].astype(F32)).astype(BF)
    qkv[0, :, pl.ds(2 * HEAD, HEAD)] = (
        probs[:, pl.ds(0, HEAD)] + grecv[pl.ds(TOK, TOK), :].astype(F32)).astype(BF)

    pltpu.make_async_remote_copy(
        src_ref=send2, dst_ref=recv2, send_sem=s2send, recv_sem=s2recv,
        device_id=sib, device_id_type=MESH).wait_recv()
    acc = recv2[0].astype(F32)
    for s in range(1, 32):
        acc = acc + recv2[s].astype(F32)
    bucket[...] = acc[:25] * (1.0 / math.sqrt(65536))

    for c in sent:
        c.wait_send()

    def drain(count):
        pltpu.make_async_remote_copy(
            src_ref=send2.at[pl.ds(0, count)], dst_ref=recv2.at[pl.ds(0, count)],
            send_sem=s2send, recv_sem=s2recv, device_id=sib, device_id_type=MESH).wait_send()

    @pl.when(mine)
    def _():
        drain(31)

    @pl.when(jnp.logical_not(mine))
    def _():
        drain(32)


def per_device(queries, keys, values, out_grad, out_weight, block_offsets):
    hbm = pl.BlockSpec(memory_space=pltpu.HBM)
    vmem = pl.BlockSpec(memory_space=pltpu.VMEM)
    messages = 96
    bucket, qkv = pl.pallas_call(
        kernel,
        out_shape=(pltpu.VMEM((25, 128), F32), pltpu.VMEM((1, TOK, 3 * HEAD), BF)),
        in_specs=[hbm] * 6,
        out_specs=(vmem, vmem),
        scratch_shapes=[
            pltpu.VMEM((2 * TOK, WIDTH), BF),
            pltpu.VMEM((16, HEAD, COLS), BF),
            pltpu.VMEM((GROWS, 128), F32),
            pltpu.VMEM((2, 408, 128), F32),
            pltpu.VMEM((2, 8, CHUNK, 128), BF),
            pltpu.VMEM((2, 2, 7, 208, 128), BF),
            pltpu.VMEM((HEAD + 8, 2 * TOK), F32),
            pltpu.VMEM((TOK, HEAD), BF),
            pltpu.VMEM((2 * TOK, HEAD), BF),
            pltpu.VMEM((2 * TOK, HEAD), BF),
            pltpu.VMEM((TOK, 2 * TOK), F32),
            pltpu.VMEM((TOK, HEAD), F32),
            pltpu.VMEM((2 * TOK, HEAD), BF),
            pltpu.VMEM((2 * TOK, HEAD), BF),
            pltpu.VMEM((32, 32, 128), BF),
            pltpu.VMEM((32, 32, 128), BF),
            pltpu.SMEM((129,), jnp.int32),
            pltpu.SMEM((160,), jnp.int32),
            pltpu.SMEM((4, 128), jnp.int32),
            pltpu.SemaphoreType.DMA((6,)),
            pltpu.SemaphoreType.DMA((messages,)),
            pltpu.SemaphoreType.DMA((messages,)),
            pltpu.SemaphoreType.DMA,
            pltpu.SemaphoreType.DMA,
        ],
        compiler_params=pltpu.CompilerParams(
            collective_id=0, has_side_effects=True, vmem_limit_bytes=60 << 20),
        name="attention_backward",
    )(queries, keys, values, out_grad, out_weight, block_offsets)
    return bucket.reshape(3200), qkv


def solution(mesh):
    return jax.shard_map(
        per_device,
        mesh=mesh,
        in_specs=(
            P("group", "node", None),
            P("group", "node", None),
            P("group", "node", None),
            P("group", "node", None),
            P(None, "node"),
            P(),
        ),
        out_specs=(P(("node", "group")), P("group", "node", None)),
        check_vma=False,
    )
```

```python
import math

import jax
import jax.numpy as jnp
from jax import lax
from jax.experimental import pallas as pl
from jax.experimental.pallas import tpu as pltpu
from jax.sharding import PartitionSpec as P

MESH = pl.DeviceIdType.MESH
BF = jnp.bfloat16
F32 = jnp.float32

HEAD = 128
TOK = 128
WIDTH = 12288
COLS = 768
PER = 96
NB = 80
B0 = 56
PAD = 56
STEP = 97
GROWS = PAD + NB * STEP + PAD
WIN = 50
CHUNK = 400
PARTS = ((0, 112), (112, 96), (208, 96), (304, 96))
OCH = 6
OW = WIDTH // OCH

STEPS = ((-4, -2), (-3, -1), (3, 1), (-1, -1), (1, 1), (-2, -2), (2, 2))


def dot(a, b, ca, cb):
    return lax.dot_general(a, b, (((ca,), (cb,)), ((), ())), preferred_element_type=F32)


def kernel(q_hbm, k_hbm, v_hbm, o_hbm, w_hbm, off_hbm, bucket, qkv,
           O, W, G, F, S, R, At, q, K, V, probs, hg, gsend, grecv, send2, recv2, off, first, tab,
           lsem, ssem, rsem, s2send, s2recv):
    node = lax.axis_index("node")
    group = lax.axis_index("group")
    x, zlo = node // 4, node % 4
    y, zhi, k = group // 4, (group % 4) // 2, group % 2
    z = zhi * 4 + zlo

    def did(dx, dy, dz, dc):
        dx, dy, dz = (dx + 8) & 3, (dy + 16) & 7, (dz + 16) & 7
        return (dx * 4 + (dz & 3), dy * 4 + (dz >> 2) * 2 + dc)

    sib = did(x, y, z, 1 - k)
    nxt = (lax.rem(node + 1, 16), group)
    prv = (lax.rem(node + 15, 16), group)
    counter = [0]

    def send(src, dst, dev, only=None):
        i = counter[0]
        counter[0] += 1
        cp = pltpu.make_async_remote_copy(
            src_ref=src, dst_ref=dst, send_sem=ssem.at[i], recv_sem=rsem.at[i],
            device_id=dev, device_id_type=MESH)
        if only is None:
            cp.start()
        else:
            pl.when(only)(cp.start)
        sent.append((cp, only))
        return cp

    sent = []

    bar = pltpu.get_barrier_semaphore()
    chip_line = [did(x + dx, y, z, dc) for dx in range(4) for dc in (k, 1 - k)][1:]
    near = [prv] + [did(x, y + d, z, k) for d in (1, -1, 2, -2)] + [did(x, y, z + d, k) for d in (1, -1, 2, -2)] + chip_line
    for dev in near:
        pl.semaphore_signal(bar, inc=1, device_id=dev, device_id_type=MESH)
    src_core = x // 2
    mine = src_core == k

    own_rows = pl.ds(pl.multiple_of(TOK * k, TOK), TOK)
    locals_ = [
        pltpu.make_async_copy(q_hbm.at[0], q, lsem.at[0]),
        pltpu.make_async_copy(k_hbm.at[0], K.at[pl.ds(TOK, TOK)], lsem.at[1]),
        pltpu.make_async_copy(v_hbm.at[0], V.at[pl.ds(TOK, TOK)], lsem.at[2]),
        pltpu.make_async_copy(o_hbm.at[0], O.at[own_rows], lsem.at[3]),
        pltpu.make_async_copy(w_hbm, W.at[node], lsem.at[4]),
        pltpu.make_async_copy(off_hbm, off, lsem.at[5]),
    ]
    for c in locals_:
        c.start()

    rows8 = lax.broadcasted_iota(jnp.int32, (8, 2 * TOK), 0)
    At[pl.ds(HEAD, 8), :] = jnp.where(rows8 == 0, 1.0, 0.0)

    nothing = jnp.zeros((TOK, HEAD), BF)

    @pl.when(node == 0)
    def _():
        K[pl.ds(0, TOK), :] = nothing
        V[pl.ds(0, TOK), :] = nothing

    @pl.when(node == 15)
    def _():
        grecv[pl.ds(0, TOK), :] = nothing
        grecv[pl.ds(TOK, TOK), :] = nothing

    pl.semaphore_wait(bar, len(near))

    cp_k = send(k_hbm.at[0], K.at[pl.ds(0, TOK)], nxt, node < 15)
    cp_v = send(v_hbm.at[0], V.at[pl.ds(0, TOK)], nxt, node < 15)

    half = pl.multiple_of(64 * k, 64)

    def nbr(axis, delta):
        return did(x, y, z + delta, k) if axis == 0 else did(x + delta, y, z, k)

    def nid(a, b):
        return ((x + b + 4) & 3) * 4 + ((zlo + a + 4) & 3)

    def wpart(n):
        return W.at[n, pl.ds(half, 64)]

    def relay(n, e):
        part = W.at[n, pl.ds(half + (0 if e == 1 else 32), 32)]
        return send(part, part, nbr(relay_axis[0], e))

    relay_axis = [0]

    def spread(a, src):
        for e in (1, -1):
            m2[a, e] = send(src, wpart(nid(a, 0)), nbr(1, e))

    def share(a, b):
        wsib[a, b] = send(wpart(nid(a, b)), wpart(nid(a, b)), sib)

    def first_near():
        relay_axis[0] = 0
        for e in (1, -1):
            m1[e].wait_recv()
            f1[e] = relay(nid(-e, 0), e)
        for a in (-1, 1):
            spread(a, wpart(nid(a, 0)))
            share(a, 0)

    def first_far():
        for e in (1, -1):
            f1[e].wait_recv()
        spread(2, wpart(nid(2, 0)))
        share(2, 0)

    def second_near(a):
        relay_axis[0] = 1
        for e in (1, -1):
            m2[a, e].wait_recv()
            f2[a, e] = relay(nid(a, -e), e)
        for b in (-1, 1):
            share(a, b)

    def second_far(a):
        for e in (1, -1):
            f2[a, e].wait_recv()
        share(a, 2)

    w_own = w_hbm.at[pl.ds(half, 64)]
    m1, m2, f1, f2, wsib = {}, {}, {}, {}, {}
    cp_o = [send(o_hbm.at[0, :, pl.ds(OW * j, OW)], O.at[own_rows, pl.ds(OW * j, OW)], sib)
            for j in range(OCH)]

    b0 = B0 * k
    locals_[5].wait()
    for i in range(8):
        first[i] = -100000
        first[137 + i] = 100000

    def rows_of(i, carry):
        first[8 + i] = lax.shift_right_logical(off[i], 7)
        return carry
    lax.fori_loop(0, 129, rows_of, 0, unroll=43)

    def table(w):
        f0 = 6400 * k + WIN * w
        low = lax.shift_right_logical((f0 - 416 + 8 * PER) * 43691, 22)
        at = low
        for j in range(1, 6):
            at = at + (first[low + j] <= f0).astype(jnp.int32)
        a, b = first[at] - f0, first[at + 1] - f0
        base = PAD + (at - 8 - b0) * STEP
        tab[0, w] = base + jnp.minimum(-a, PER)
        tab[1, w] = base + STEP - jnp.clip(b, 0, PAD)
        tab[2, w] = a + PER
        tab[3, w] = b

    for w in range(48):
        table(w)
    for e in (1, -1):
        m1[e] = send(w_own, wpart(node), nbr(0, e))
    spread(0, w_own)
    for w in range(48, 128):
        table(w)
    for c in locals_[:3]:
        c.wait()
    @pl.when(node > 0)
    def _():
        cp_k.wait_recv()
        cp_v.wait_recv()
    scale = 1.0 / math.sqrt(HEAD)
    scores = dot(q[...], K[...], 1, 1) * scale
    rp = lax.broadcasted_iota(jnp.int32, (TOK, 2 * TOK), 0)
    cpos = lax.broadcasted_iota(jnp.int32, (TOK, 2 * TOK), 1)
    lowest = jnp.where(node == 0, TOK, 0)
    allowed = (cpos > rp) & (cpos <= rp + TOK) & (cpos >= lowest)
    scores = jnp.where(allowed, scores, -jnp.inf)
    top = jnp.max(scores, axis=1, keepdims=True)
    expo = jnp.exp(scores - top)
    pr = expo / jnp.sum(expo, axis=1, keepdims=True)
    probs[...] = pr
    att = dot(pr.astype(BF), V[...], 1, 0)
    att_cols = pl.ds(pl.multiple_of(TOK * k, TOK), TOK)
    At[pl.ds(0, HEAD), att_cols] = jnp.transpose(att)
    cp_a = send(At.at[pl.ds(0, HEAD), att_cols], At.at[pl.ds(0, HEAD), att_cols], sib)
    first_near()

    cp_a.wait_recv()
    locals_[3].wait()
    lhs = At[pl.ds(pl.multiple_of(b0, 8), NB), :].astype(BF)

    for t in range(WIDTH // 256):
        if t % (OW // 256) == 0:
            cp_o[t // (OW // 256)].wait_recv()
        prod = dot(lhs, O[:, pl.ds(256 * t, 256)], 1, 0)
        G[pl.ds(PAD + 2 * t, NB, stride=STEP), :] = prod[:, :128]
        G[pl.ds(PAD + 2 * t + 1, NB, stride=STEP), :] = prod[:, 128:]

    rwin = lax.broadcasted_iota(jnp.int32, (56, 128), 0)

    def gather(delta):
        for a, p in ((0, y), (1, z)):
            d = (p + delta + 16) & 7
            for m in range(8):
                if a == 0:
                    w = 16 * (m % 4) + 2 * d + m // 4
                else:
                    w = 64 + 16 * (d & 3) + 2 * m + (d >> 2)
                one = G[pl.ds(tab[0, w], 56), :]
                two = G[pl.ds(tab[1, w], 56), :]
                F[a, pl.ds(WIN * m, 56), :] = jnp.where(
                    rwin < tab[2, w], one, jnp.where(rwin >= tab[3, w], two, 0.0))
            S[a, d] = F[a, pl.ds(0, CHUNK), :].astype(BF)

    msgs = {}

    def ring(h, m, parts=()):
        lo, size = PARTS[h]
        sign = 1 - 2 * (h % 2)
        owner, target = STEPS[m]
        rows = pl.ds(lo, size)
        for a, p in ((0, y), (1, z)):
            d = (p + sign * owner + 16) & 7
            if parts:
                total = S[a, d, rows].astype(F32)
                for i in parts:
                    msgs[a, h, i].wait_recv()
                    total = total + R[a, h, i, pl.ds(0, size)].astype(F32)
                S[a, d, rows] = total.astype(BF)
            t = sign * target
            to = did(x, y + t, z, k) if a == 0 else did(x, y, z + t, k)
            msgs[a, h, m] = send(S.at[a, d, rows], R.at[a, h, m, pl.ds(0, size)], to)

    for delta in (4, -3, 3):
        gather(delta)
    for m in (0, 1, 2):
        ring(0, m)
        ring(1, m)
    for delta in (-1, 1, -2, 2, 0):
        gather(delta)
    for m in (0, 1, 2):
        ring(2, m)
        ring(3, m)
    second_near(0)
    for h in range(4):
        ring(h, 3)
        ring(h, 4)
    first_far()
    second_near(-1)
    second_near(1)
    hg[...] = jnp.zeros((TOK, HEAD), F32)
    locals_[4].wait()

    def head(keys, shards):
        for key in keys:
            wsib[key].wait_recv()
        total = hg[...]
        for dx, dz in shards:
            n = ((x + dx + 4) & 3) * 4 + ((zlo + dz + 4) & 3)
            cols = pl.ds(pl.multiple_of(COLS * n, COLS), COLS)
            total = total + dot(O[own_rows, cols], W[n], 1, 1)
        hg[...] = total

    for h in range(4):
        ring(h, 6, (2,))
        ring(h, 5, (0, 1))
    second_near(2)
    second_far(0)
    head([(1, 0), (-1, 0), (2, 0), (0, 1), (0, -1), (0, 2)],
         [(0, 0), (1, 0), (-1, 0), (2, 0), (0, 1), (0, -1), (0, 2)])
    head([(1, 1), (-1, 1), (1, -1), (-1, -1)], [(1, 1), (-1, 1), (1, -1), (-1, -1)])
    for a in (2, -1, 1):
        second_far(a)
    for h, (lo, size) in enumerate(PARTS):
        for a, p in ((0, y), (1, z)):
            total = S[a, p, pl.ds(lo, size)].astype(F32)
            for i in (3, 4, 5, 6):
                msgs[a, h, i].wait_recv()
                total = total + R[a, h, i, pl.ds(0, size)].astype(F32)
            F[a, pl.ds(lo, size), :] = total
            for i in range(4 * h, 4 * h + 4):
                send2[16 * a + i] = F[a, pl.ds(25 * i, 32), :].astype(BF)
        for i in range(4 * h, 4 * h + 4):
            r, dc = i // 2, i % 2
            for a, p in ((0, z), (1, y)):
                src, dst = send2.at[16 * a + i], recv2.at[x * 8 + p]
                to = did(2 * k + a, y, r, dc) if a == 0 else did(2 * k + a, r, z, dc)
                here = (2 * k + a == x) & (p == r) & (k == dc)

                @pl.when(jnp.logical_not(here))
                def _():
                    pltpu.make_async_remote_copy(
                        src_ref=src, dst_ref=dst, send_sem=s2send, recv_sem=s2recv,
                        device_id=to, device_id_type=MESH).start()

                @pl.when(here)
                def _():
                    pltpu.make_async_copy(src, dst, s2recv).start()

    head([(2, 1), (2, -1), (-1, 2), (1, 2), (2, 2)], [(2, 1), (2, -1), (1, 2), (-1, 2), (2, 2)])

    head_low = hg[...].astype(BF)
    prob_grad = dot(head_low, V[...], 1, 1)
    pr = probs[...]
    center = jnp.sum(pr * prob_grad, axis=1, keepdims=True)
    sg = pr * (prob_grad - center) * scale
    grad_q = dot(sg.astype(BF), K[...], 1, 0)
    kg = dot(jnp.transpose(sg).astype(BF), q[...], 1, 0)
    vg = dot(jnp.transpose(pr).astype(BF), head_low, 1, 0)
    gsend[pl.ds(0, TOK), :] = kg[:TOK].astype(BF)
    gsend[pl.ds(TOK, TOK), :] = vg[:TOK].astype(BF)
    cp_g = send(gsend, grecv, prv, node > 0)
    qkv[0, :, pl.ds(0, HEAD)] = grad_q.astype(BF)
    hg[...] = kg[TOK:]
    probs[:, pl.ds(0, HEAD)] = vg[TOK:]


    pl.when(node < 15)(cp_g.wait_recv)
    qkv[0, :, pl.ds(HEAD, HEAD)] = (hg[...] + grecv[pl.ds(0, TOK), :].astype(F32)).astype(BF)
    qkv[0, :, pl.ds(2 * HEAD, HEAD)] = (
        probs[:, pl.ds(0, HEAD)] + grecv[pl.ds(TOK, TOK), :].astype(F32)).astype(BF)

    pltpu.make_async_remote_copy(
        src_ref=send2, dst_ref=recv2, send_sem=s2send, recv_sem=s2recv,
        device_id=sib, device_id_type=MESH).wait_recv()
    acc = recv2[0].astype(F32)
    for s in range(1, 32):
        acc = acc + recv2[s].astype(F32)
    bucket[...] = acc[:25] * (1.0 / math.sqrt(65536))

    for c, only in sent:
        if only is None:
            c.wait_send()
        else:
            pl.when(only)(c.wait_send)

    def drain(count):
        pltpu.make_async_remote_copy(
            src_ref=send2.at[pl.ds(0, count)], dst_ref=recv2.at[pl.ds(0, count)],
            send_sem=s2send, recv_sem=s2recv, device_id=sib, device_id_type=MESH).wait_send()

    @pl.when(mine)
    def _():
        drain(31)

    @pl.when(jnp.logical_not(mine))
    def _():
        drain(32)


def per_device(queries, keys, values, out_grad, out_weight, block_offsets):
    hbm = pl.BlockSpec(memory_space=pltpu.HBM)
    vmem = pl.BlockSpec(memory_space=pltpu.VMEM)
    messages = 128
    bucket, qkv = pl.pallas_call(
        kernel,
        out_shape=(pltpu.VMEM((25, 128), F32), pltpu.VMEM((1, TOK, 3 * HEAD), BF)),
        in_specs=[hbm] * 6,
        out_specs=(vmem, vmem),
        scratch_shapes=[
            pltpu.VMEM((2 * TOK, WIDTH), BF),
            pltpu.VMEM((16, HEAD, COLS), BF),
            pltpu.VMEM((GROWS, 128), F32),
            pltpu.VMEM((2, 408, 128), F32),
            pltpu.VMEM((2, 8, CHUNK, 128), BF),
            pltpu.VMEM((2, 4, 7, 112, 128), BF),
            pltpu.VMEM((HEAD + 8, 2 * TOK), F32),
            pltpu.VMEM((TOK, HEAD), BF),
            pltpu.VMEM((2 * TOK, HEAD), BF),
            pltpu.VMEM((2 * TOK, HEAD), BF),
            pltpu.VMEM((TOK, 2 * TOK), F32),
            pltpu.VMEM((TOK, HEAD), F32),
            pltpu.VMEM((2 * TOK, HEAD), BF),
            pltpu.VMEM((2 * TOK, HEAD), BF),
            pltpu.VMEM((32, 32, 128), BF),
            pltpu.VMEM((32, 32, 128), BF),
            pltpu.SMEM((129,), jnp.int32),
            pltpu.SMEM((160,), jnp.int32),
            pltpu.SMEM((4, 128), jnp.int32),
            pltpu.SemaphoreType.DMA((6,)),
            pltpu.SemaphoreType.DMA((messages,)),
            pltpu.SemaphoreType.DMA((messages,)),
            pltpu.SemaphoreType.DMA,
            pltpu.SemaphoreType.DMA,
        ],
        compiler_params=pltpu.CompilerParams(
            collective_id=0, has_side_effects=True, vmem_limit_bytes=60 << 20),
        name="attention_backward",
    )(queries, keys, values, out_grad, out_weight, block_offsets)
    return bucket.reshape(3200), qkv


def solution(mesh):
    return jax.shard_map(
        per_device,
        mesh=mesh,
        in_specs=(
            P("group", "node", None),
            P("group", "node", None),
            P("group", "node", None),
            P("group", "node", None),
            P(None, "node"),
            P(),
        ),
        out_specs=(P(("node", "group")), P("group", "node", None)),
        check_vma=False,
    )
```

```python
import math

import jax
import jax.numpy as jnp
from jax import lax
from jax.experimental import pallas as pl
from jax.experimental.pallas import tpu as pltpu
from jax.sharding import PartitionSpec as P

MESH = pl.DeviceIdType.MESH
BF = jnp.bfloat16
F32 = jnp.float32

HEAD = 128
TOK = 128
WIDTH = 12288
COLS = 768
PER = 96
NB = 80
B0 = 56
PAD = 56
STEP = 97
GROWS = PAD + NB * STEP + PAD
WIN = 50
CHUNK = 400
PARTS = ((0, 112), (112, 96), (208, 96), (304, 96))
OCH = 6
OW = WIDTH // OCH

STEPS = ((-4, -2), (-3, -1), (3, 1), (-1, -1), (1, 1), (-2, -2), (2, 2))


def dot(a, b, ca, cb):
    return lax.dot_general(a, b, (((ca,), (cb,)), ((), ())), preferred_element_type=F32)


def kernel(q_hbm, k_hbm, v_hbm, o_hbm, w_hbm, off_hbm, bucket, qkv,
           O, W, G, F, S, R, At, q, K, V, probs, hg, gsend, grecv, send2, recv2, off, first, tab,
           lsem, ssem, rsem, s2send, s2recv):
    node = lax.axis_index("node")
    group = lax.axis_index("group")
    x, zlo = node // 4, node % 4
    y, zhi, k = group // 4, (group % 4) // 2, group % 2
    z = zhi * 4 + zlo

    def did(dx, dy, dz, dc):
        dx, dy, dz = (dx + 8) & 3, (dy + 16) & 7, (dz + 16) & 7
        return (dx * 4 + (dz & 3), dy * 4 + (dz >> 2) * 2 + dc)

    sib = did(x, y, z, 1 - k)
    nxt = (lax.rem(node + 1, 16), group)
    prv = (lax.rem(node + 15, 16), group)
    counter = [0]

    def send(src, dst, dev, only=None):
        i = counter[0]
        counter[0] += 1
        cp = pltpu.make_async_remote_copy(
            src_ref=src, dst_ref=dst, send_sem=ssem.at[i], recv_sem=rsem.at[i],
            device_id=dev, device_id_type=MESH)
        if only is None:
            cp.start()
        else:
            pl.when(only)(cp.start)
        sent.append((cp, only))
        return cp

    sent = []

    bar = pltpu.get_barrier_semaphore()
    chip_line = [did(x + dx, y, z, dc) for dx in range(4) for dc in (k, 1 - k)][1:]
    near = [prv] + [did(x, y + d, z, k) for d in (1, -1, 2, -2)] + [did(x, y, z + d, k) for d in (1, -1, 2, -2)] + chip_line
    for dev in near:
        pl.semaphore_signal(bar, inc=1, device_id=dev, device_id_type=MESH)
    src_core = x // 2
    mine = src_core == k

    own_rows = pl.ds(pl.multiple_of(TOK * k, TOK), TOK)
    locals_ = [
        pltpu.make_async_copy(q_hbm.at[0], q, lsem.at[0]),
        pltpu.make_async_copy(k_hbm.at[0], K.at[pl.ds(TOK, TOK)], lsem.at[1]),
        pltpu.make_async_copy(v_hbm.at[0], V.at[pl.ds(TOK, TOK)], lsem.at[2]),
        pltpu.make_async_copy(o_hbm.at[0], O.at[own_rows], lsem.at[3]),
        pltpu.make_async_copy(w_hbm, W.at[node], lsem.at[4]),
        pltpu.make_async_copy(off_hbm, off, lsem.at[5]),
    ]
    for c in locals_:
        c.start()

    rows8 = lax.broadcasted_iota(jnp.int32, (8, 2 * TOK), 0)
    At[pl.ds(HEAD, 8), :] = jnp.where(rows8 == 0, 1.0, 0.0)

    nothing = jnp.zeros((TOK, HEAD), BF)

    @pl.when(node == 0)
    def _():
        K[pl.ds(0, TOK), :] = nothing
        V[pl.ds(0, TOK), :] = nothing

    @pl.when(node == 15)
    def _():
        grecv[pl.ds(0, TOK), :] = nothing
        grecv[pl.ds(TOK, TOK), :] = nothing

    pl.semaphore_wait(bar, len(near))

    cp_k = send(k_hbm.at[0], K.at[pl.ds(0, TOK)], nxt, node < 15)
    cp_v = send(v_hbm.at[0], V.at[pl.ds(0, TOK)], nxt, node < 15)

    half = pl.multiple_of(64 * k, 64)

    def nbr(axis, delta):
        return did(x, y, z + delta, k) if axis == 0 else did(x + delta, y, z, k)

    def nid(a, b):
        return ((x + b + 4) & 3) * 4 + ((zlo + a + 4) & 3)

    def wpart(n):
        return W.at[n, pl.ds(half, 64)]

    def relay(n, e):
        part = W.at[n, pl.ds(half + (0 if e == 1 else 32), 32)]
        return send(part, part, nbr(relay_axis[0], e))

    relay_axis = [0]

    def spread(a, src):
        for e in (1, -1):
            m2[a, e] = send(src, wpart(nid(a, 0)), nbr(1, e))

    def share(a, b):
        wsib[a, b] = send(wpart(nid(a, b)), wpart(nid(a, b)), sib)

    def first_near():
        relay_axis[0] = 0
        for e in (1, -1):
            m1[e].wait_recv()
            f1[e] = relay(nid(-e, 0), e)
        for a in (-1, 1):
            spread(a, wpart(nid(a, 0)))
            share(a, 0)

    def first_far():
        for e in (1, -1):
            f1[e].wait_recv()
        spread(2, wpart(nid(2, 0)))
        share(2, 0)

    def second_near(a):
        relay_axis[0] = 1
        for e in (1, -1):
            m2[a, e].wait_recv()
            f2[a, e] = relay(nid(a, -e), e)
        for b in (-1, 1):
            share(a, b)

    def second_far(a):
        for e in (1, -1):
            f2[a, e].wait_recv()
        share(a, 2)

    w_own = w_hbm.at[pl.ds(half, 64)]
    m1, m2, f1, f2, wsib = {}, {}, {}, {}, {}
    cp_o = [send(o_hbm.at[0, :, pl.ds(OW * j, OW)], O.at[own_rows, pl.ds(OW * j, OW)], sib)
            for j in range(OCH)]

    b0 = B0 * k
    locals_[5].wait()
    for i in range(8):
        first[i] = -100000
        first[137 + i] = 100000

    def rows_of(i, carry):
        first[8 + i] = lax.shift_right_logical(off[i], 7)
        return carry
    lax.fori_loop(0, 129, rows_of, 0, unroll=43)

    def table(w):
        f0 = 6400 * k + WIN * w
        low = lax.shift_right_logical((f0 - 416 + 8 * PER) * 43691, 22)
        at = low
        for j in range(1, 6):
            at = at + (first[low + j] <= f0).astype(jnp.int32)
        a, b = first[at] - f0, first[at + 1] - f0
        base = PAD + (at - 8 - b0) * STEP
        tab[0, w] = base + jnp.minimum(-a, PER)
        tab[1, w] = base + STEP - jnp.clip(b, 0, PAD)
        tab[2, w] = a + PER
        tab[3, w] = b

    for w in range(48):
        table(w)
    for e in (1, -1):
        m1[e] = send(w_own, wpart(node), nbr(0, e))
    spread(0, w_own)
    for w in range(48, 128):
        table(w)
    for c in locals_[:3]:
        c.wait()
    @pl.when(node > 0)
    def _():
        cp_k.wait_recv()
        cp_v.wait_recv()
    scale = 1.0 / math.sqrt(HEAD)
    scores = dot(q[...], K[...], 1, 1) * scale
    rp = lax.broadcasted_iota(jnp.int32, (TOK, 2 * TOK), 0)
    cpos = lax.broadcasted_iota(jnp.int32, (TOK, 2 * TOK), 1)
    lowest = jnp.where(node == 0, TOK, 0)
    allowed = (cpos > rp) & (cpos <= rp + TOK) & (cpos >= lowest)
    scores = jnp.where(allowed, scores, -jnp.inf)
    top = jnp.max(scores, axis=1, keepdims=True)
    expo = jnp.exp(scores - top)
    pr = expo / jnp.sum(expo, axis=1, keepdims=True)
    probs[...] = pr
    att = dot(pr.astype(BF), V[...], 1, 0)
    att_cols = pl.ds(pl.multiple_of(TOK * k, TOK), TOK)
    At[pl.ds(0, HEAD), att_cols] = jnp.transpose(att)
    cp_a = send(At.at[pl.ds(0, HEAD), att_cols], At.at[pl.ds(0, HEAD), att_cols], sib)
    first_near()

    cp_a.wait_recv()
    locals_[3].wait()
    lhs = At[pl.ds(pl.multiple_of(b0, 8), NB), :].astype(BF)

    for t in range(WIDTH // 256):
        if t % (OW // 256) == 0:
            cp_o[t // (OW // 256)].wait_recv()
        prod = dot(lhs, O[:, pl.ds(256 * t, 256)], 1, 0)
        G[pl.ds(PAD + 2 * t, NB, stride=STEP), :] = prod[:, :128]
        G[pl.ds(PAD + 2 * t + 1, NB, stride=STEP), :] = prod[:, 128:]

    rwin = lax.broadcasted_iota(jnp.int32, (56, 128), 0)

    def gather(delta):
        for a, p in ((0, y), (1, z)):
            d = (p + delta + 16) & 7
            for m in range(8):
                if a == 0:
                    w = 16 * (m % 4) + 2 * d + m // 4
                else:
                    w = 64 + 16 * (d & 3) + 2 * m + (d >> 2)
                one = G[pl.ds(tab[0, w], 56), :]
                two = G[pl.ds(tab[1, w], 56), :]
                F[a, pl.ds(WIN * m, 56), :] = jnp.where(
                    rwin < tab[2, w], one, jnp.where(rwin >= tab[3, w], two, 0.0))
            S[a, d] = F[a, pl.ds(0, CHUNK), :].astype(BF)

    msgs = {}

    def ring(h, m, parts=()):
        lo, size = PARTS[h]
        sign = 1 - 2 * (h % 2)
        owner, target = STEPS[m]
        rows = pl.ds(lo, size)
        for a, p in ((0, y), (1, z)):
            d = (p + sign * owner + 16) & 7
            if parts:
                total = S[a, d, rows].astype(F32)
                for i in parts:
                    msgs[a, h, i].wait_recv()
                    total = total + R[a, h, i, pl.ds(0, size)].astype(F32)
                S[a, d, rows] = total.astype(BF)
            t = sign * target
            to = did(x, y + t, z, k) if a == 0 else did(x, y, z + t, k)
            msgs[a, h, m] = send(S.at[a, d, rows], R.at[a, h, m, pl.ds(0, size)], to)

    for delta in (4, -3, 3):
        gather(delta)
    for m in (0, 1, 2):
        ring(0, m)
        ring(1, m)
    for delta in (-1, 1, -2, 2, 0):
        gather(delta)
    for m in (0, 1, 2):
        ring(2, m)
        ring(3, m)
    second_near(0)
    first_far()
    second_near(-1)
    second_near(1)
    hg[...] = jnp.zeros((TOK, HEAD), F32)
    locals_[4].wait()

    def head(keys, shards):
        for key in keys:
            wsib[key].wait_recv()
        total = hg[...]
        for dx, dz in shards:
            n = ((x + dx + 4) & 3) * 4 + ((zlo + dz + 4) & 3)
            cols = pl.ds(pl.multiple_of(COLS * n, COLS), COLS)
            total = total + dot(O[own_rows, cols], W[n], 1, 1)
        hg[...] = total

    for h in (0, 1):
        ring(h, 6, (2,))
        ring(h, 5, (0, 1))
    for h in (0, 1):
        ring(h, 3)
        ring(h, 4)
    for h in (2, 3):
        ring(h, 6, (2,))
        ring(h, 5, (0, 1))
    for h in (2, 3):
        ring(h, 3)
        ring(h, 4)
    second_near(2)
    second_far(0)
    head([(1, 0), (-1, 0), (2, 0), (0, 1), (0, -1), (0, 2)],
         [(0, 0), (1, 0), (-1, 0), (2, 0), (0, 1), (0, -1), (0, 2)])
    head([(1, 1), (-1, 1), (1, -1), (-1, -1)], [(1, 1), (-1, 1), (1, -1), (-1, -1)])
    for a in (2, -1, 1):
        second_far(a)
    for h, (lo, size) in enumerate(PARTS):
        for a, p in ((0, y), (1, z)):
            total = S[a, p, pl.ds(lo, size)].astype(F32)
            for i in (3, 4, 5, 6):
                msgs[a, h, i].wait_recv()
                total = total + R[a, h, i, pl.ds(0, size)].astype(F32)
            F[a, pl.ds(lo, size), :] = total
            for i in range(4 * h, 4 * h + 4):
                send2[16 * a + i] = F[a, pl.ds(25 * i, 32), :].astype(BF)
        for i in range(4 * h, 4 * h + 4):
            r, dc = i // 2, i % 2
            for a, p in ((0, z), (1, y)):
                src, dst = send2.at[16 * a + i], recv2.at[x * 8 + p]
                to = did(2 * k + a, y, r, dc) if a == 0 else did(2 * k + a, r, z, dc)
                here = (2 * k + a == x) & (p == r) & (k == dc)

                @pl.when(jnp.logical_not(here))
                def _():
                    pltpu.make_async_remote_copy(
                        src_ref=src, dst_ref=dst, send_sem=s2send, recv_sem=s2recv,
                        device_id=to, device_id_type=MESH).start()

                @pl.when(here)
                def _():
                    pltpu.make_async_copy(src, dst, s2recv).start()

    head([(2, 1), (2, -1), (-1, 2), (1, 2), (2, 2)], [(2, 1), (2, -1), (1, 2), (-1, 2), (2, 2)])

    head_low = hg[...].astype(BF)
    prob_grad = dot(head_low, V[...], 1, 1)
    pr = probs[...]
    center = jnp.sum(pr * prob_grad, axis=1, keepdims=True)
    sg = pr * (prob_grad - center) * scale
    grad_q = dot(sg.astype(BF), K[...], 1, 0)
    kg = dot(jnp.transpose(sg).astype(BF), q[...], 1, 0)
    vg = dot(jnp.transpose(pr).astype(BF), head_low, 1, 0)
    gsend[pl.ds(0, TOK), :] = kg[:TOK].astype(BF)
    gsend[pl.ds(TOK, TOK), :] = vg[:TOK].astype(BF)
    cp_g = send(gsend, grecv, prv, node > 0)
    qkv[0, :, pl.ds(0, HEAD)] = grad_q.astype(BF)
    hg[...] = kg[TOK:]
    probs[:, pl.ds(0, HEAD)] = vg[TOK:]


    pl.when(node < 15)(cp_g.wait_recv)
    qkv[0, :, pl.ds(HEAD, HEAD)] = (hg[...] + grecv[pl.ds(0, TOK), :].astype(F32)).astype(BF)
    qkv[0, :, pl.ds(2 * HEAD, HEAD)] = (
        probs[:, pl.ds(0, HEAD)] + grecv[pl.ds(TOK, TOK), :].astype(F32)).astype(BF)

    pltpu.make_async_remote_copy(
        src_ref=send2, dst_ref=recv2, send_sem=s2send, recv_sem=s2recv,
        device_id=sib, device_id_type=MESH).wait_recv()
    acc = recv2[0].astype(F32)
    for s in range(1, 32):
        acc = acc + recv2[s].astype(F32)
    bucket[...] = acc[:25] * (1.0 / math.sqrt(65536))

    for c, only in sent:
        if only is None:
            c.wait_send()
        else:
            pl.when(only)(c.wait_send)

    def drain(count):
        pltpu.make_async_remote_copy(
            src_ref=send2.at[pl.ds(0, count)], dst_ref=recv2.at[pl.ds(0, count)],
            send_sem=s2send, recv_sem=s2recv, device_id=sib, device_id_type=MESH).wait_send()

    @pl.when(mine)
    def _():
        drain(31)

    @pl.when(jnp.logical_not(mine))
    def _():
        drain(32)


def per_device(queries, keys, values, out_grad, out_weight, block_offsets):
    hbm = pl.BlockSpec(memory_space=pltpu.HBM)
    vmem = pl.BlockSpec(memory_space=pltpu.VMEM)
    messages = 128
    bucket, qkv = pl.pallas_call(
        kernel,
        out_shape=(pltpu.VMEM((25, 128), F32), pltpu.VMEM((1, TOK, 3 * HEAD), BF)),
        in_specs=[hbm] * 6,
        out_specs=(vmem, vmem),
        scratch_shapes=[
            pltpu.VMEM((2 * TOK, WIDTH), BF),
            pltpu.VMEM((16, HEAD, COLS), BF),
            pltpu.VMEM((GROWS, 128), F32),
            pltpu.VMEM((2, 408, 128), F32),
            pltpu.VMEM((2, 8, CHUNK, 128), BF),
            pltpu.VMEM((2, 4, 7, 112, 128), BF),
            pltpu.VMEM((HEAD + 8, 2 * TOK), F32),
            pltpu.VMEM((TOK, HEAD), BF),
            pltpu.VMEM((2 * TOK, HEAD), BF),
            pltpu.VMEM((2 * TOK, HEAD), BF),
            pltpu.VMEM((TOK, 2 * TOK), F32),
            pltpu.VMEM((TOK, HEAD), F32),
            pltpu.VMEM((2 * TOK, HEAD), BF),
            pltpu.VMEM((2 * TOK, HEAD), BF),
            pltpu.VMEM((32, 32, 128), BF),
            pltpu.VMEM((32, 32, 128), BF),
            pltpu.SMEM((129,), jnp.int32),
            pltpu.SMEM((160,), jnp.int32),
            pltpu.SMEM((4, 128), jnp.int32),
            pltpu.SemaphoreType.DMA((6,)),
            pltpu.SemaphoreType.DMA((messages,)),
            pltpu.SemaphoreType.DMA((messages,)),
            pltpu.SemaphoreType.DMA,
            pltpu.SemaphoreType.DMA,
        ],
        compiler_params=pltpu.CompilerParams(
            collective_id=0, has_side_effects=True, vmem_limit_bytes=60 << 20),
        name="attention_backward",
    )(queries, keys, values, out_grad, out_weight, block_offsets)
    return bucket.reshape(3200), qkv


def solution(mesh):
    return jax.shard_map(
        per_device,
        mesh=mesh,
        in_specs=(
            P("group", "node", None),
            P("group", "node", None),
            P("group", "node", None),
            P("group", "node", None),
            P(None, "node"),
            P(),
        ),
        out_specs=(P(("node", "group")), P("group", "node", None)),
        check_vma=False,
    )
```
